32 devices in a mesh: groups: 2 (over y), ctx: 4 (over x, core), tp: 4 (over z).
Axes of the slice: x: 2, y: 2, z: 4, core: 2. Of those that a mesh axis runs over, the one named last changes fastest.
Arguments:
- queries: bfloat16 [2048, 4096], P(('groups', 'ctx'), 'tp'), parts along dimension 0, as said below
- keys: bfloat16 [2048, 1024], P(('groups', 'ctx'), 'tp'), parts along dimension 0, as said below
- values: bfloat16 [2048, 1024], P(('groups', 'ctx'), 'tp'), parts along dimension 0, may hold values from -24 to 24
- teacher_residual: bfloat16 [2048, 8192], P(('groups', 'ctx'), 'tp'), parts along dimension 0, as said below
- teacher_out: bfloat16 [4096, 8192], P('tp', 'ctx'), may hold values from -0.09375 to 0.09375
- teacher_gain: float32 [8192], replicated, may hold values from 0.1 to 1.9
- projector: bfloat16 [8192, 3072], P('tp'), may hold values from -0.0625 to 0.0625
- span_starts: int32 [2048], P(('groups', 'ctx')), parts along dimension 0, may hold values from 0 to 1023, as said below
- span_ends: int32 [2048], P(('groups', 'ctx')), parts along dimension 0, may hold values from 1 to 1024, as said below
- aligned_counts: int32 [8], P(('groups', 'ctx')), parts along dimension 0, may hold values from 128 to 256, as said below
- student_context: bfloat16 [2048, 3072], P(('groups', 'ctx'), 'tp'), parts along dimension 0, may hold values from -0.75 to 0.75
- student_out: bfloat16 [3072, 3072], P('tp'), may hold values from -0.109375 to 0.109375
- student_residual: bfloat16 [2048, 3072], P(('groups', 'ctx'), 'tp'), parts along dimension 0, may hold values from -1.5 to 1.5
Outputs:
- grad_out: float32 [6144, 3072], P(('groups', 'tp'), 'ctx'), parts along dimension 0
- grad_context: bfloat16 [2048, 3072], P(('groups', 'ctx'), 'tp'), parts along dimension 0
The draws below stay inside these ranges and needn't reach their ends.
There are 2 independent parts, one for each index of `groups`. The reference program is written for one: setup_inputs(seed, part) draws one part's arguments, and reference() takes and returns one part's arrays. A program takes and returns all parts, laid end to end along the dimension named above; an argument that names none is the same for every part. Nothing has to cross between parts.
Inputs may be any that keep to these rules, and one draw needn't show every extreme that they name: `queries`: entries lie within -12 to 12. `keys`: entries lie within -12 to 12. `teacher_residual`: entries lie within -8 to 8. Student token s takes teacher rows span_starts[s] to span_ends[s] - 1; span_starts[s] lies in s - 16 .. s (never below 0), and the first token of every shard of 256 tokens starts exactly 16 rows back where the sequence allows. span_ends[s] lies in s + 1 .. s + 1 + 16 (never above 1024); the last token of every shard of 256 tokens ends exactly 16 rows ahead where the sequence allows. Shard j's first aligned_counts[j] tokens are distilled, its later ones are not.
All inputs are finite; a program needn't handle non-finite values.
Results may differ from the reference program's by a relative error of at most 0.017.
Values may be sent and summed in bfloat16 or wider, within the bound.
A program may use at most 128 MiB of HBM per device.

```python
import math
import jax
import jax.numpy as jnp
from jax import lax

TD = 8192
HEADS = 32
KV_HEADS = 8
HEAD = 128
SD = 3072
TOK_DEV = 256
HALO = 16
TOKENS = 1024
CTX_SHARDS = 4
N_TP = 4


def shared_keys(key):
    return jnp.clip(jax.random.normal(key, (TOKENS, KV_HEADS * HEAD), jnp.float32), -2.4, 2.4)


def span_reach(key):
    before_key, after_key = jax.random.split(jax.random.fold_in(key, 101))
    positions = jnp.arange(TOKENS, dtype=jnp.int32)
    local_rows = positions % TOK_DEV
    reach_before = jax.random.randint(before_key, (TOKENS,), 0, HALO + 1, dtype=jnp.int32)
    reach_after = jax.random.randint(after_key, (TOKENS,), 0, HALO + 1, dtype=jnp.int32)
    reach_before = jnp.where(local_rows == 0, HALO, reach_before)
    reach_before = jnp.where(positions == TOKENS - 1, 0, reach_before)
    reach_after = jnp.where(local_rows == TOK_DEV - 1, HALO, reach_after)
    reach_after = jnp.where(positions == 0, 0, reach_after)
    return (reach_before, reach_after)


def draw_keys(key, part):
    shared = shared_keys(key)
    return shared.astype(jnp.bfloat16)


def draw_queries(key, part):
    key = jax.random.fold_in(key, 7)
    fresh_draw = jnp.clip(jax.random.normal(key, (TOKENS, HEADS * HEAD), jnp.float32), -2.4, 2.4)
    return fresh_draw.astype(jnp.bfloat16)


def draw_teacher_residual(key, part):
    key = jax.random.fold_in(key, 13)
    row_key, column_key, entry_key = jax.random.split(key, 3)
    row_scale = jnp.exp(jax.random.uniform(row_key, (TOKENS, 1), jnp.float32, 0.0, math.log(10.0))) / 15.0
    fraction = jnp.arange(TD, dtype=jnp.float32) / TD
    jitter = jnp.exp(jax.random.uniform(column_key, (1, TD), jnp.float32, math.log(0.8), math.log(1.25)))
    ramp = 0.3 * jnp.exp(math.log(10.0) * fraction)
    entries = jnp.clip(jax.random.normal(entry_key, (TOKENS, TD), jnp.float32), -3.0, 3.0)
    return (entries * row_scale * ramp[None, :] * jitter).astype(jnp.bfloat16)


def draw_span_starts(key, part):
    reach_before, unused_after = span_reach(key)
    positions = jnp.arange(TOKENS, dtype=jnp.int32)
    return jnp.maximum(positions - reach_before, 0).astype(jnp.int32)


def draw_span_ends(key, part):
    unused_before, reach_after = span_reach(key)
    positions = jnp.arange(TOKENS, dtype=jnp.int32)
    return jnp.minimum(positions + 1 + reach_after, TOKENS).astype(jnp.int32)


def draw_aligned_counts(key, part):
    key = jax.random.fold_in(key, 29)
    count_key, chosen_key = jax.random.split(key)
    counts_drawn = jax.random.randint(count_key, (CTX_SHARDS,), TOK_DEV // 2, TOK_DEV + 1, dtype=jnp.int32)
    chosen = jax.random.randint(chosen_key, (), 0, CTX_SHARDS, dtype=jnp.int32)
    shards = jnp.arange(CTX_SHARDS, dtype=jnp.int32)
    following = (chosen + 1) % CTX_SHARDS
    counts_drawn = jnp.where(shards == following, TOK_DEV // 2, counts_drawn)
    return jnp.where(shards == chosen, TOK_DEV, counts_drawn).astype(jnp.int32)


def block_scale(rng, shape, cuts, smallest, top_value):
    def one(axis_at, shards_of):
        steps = jax.random.uniform(jax.random.fold_in(jax.random.fold_in(rng, 6), axis_at), (shards_of,), jnp.float32, smallest / len(cuts), top_value / len(cuts))
        return jnp.repeat(jnp.exp(steps), shape[axis_at] // shards_of).reshape((-1,) + (1,) * (len(shape) - axis_at - 1))

    level = one(*cuts[0])
    for cut in cuts[1:]:
        level = level * one(*cut)
    return level


def scatter_about(rng, shape, scale, most, cuts=(), kind=jnp.bfloat16):
    factor_of = block_scale(rng, shape, cuts, -0.22, 0.18) if cuts else 1.0
    result = jax.random.normal(rng, shape, jnp.float32) * scale * factor_of
    return jnp.minimum(jnp.maximum(result, -most), most).astype(kind)


def setup_inputs(seed: int = 0, part: int = 0) -> dict:
    splits = jax.random.split(jax.random.key(seed), 14)
    part_splits = jax.random.split(jax.random.fold_in(splits[13], part), 14)
    queries = draw_queries(jax.random.fold_in(jax.random.fold_in(splits[13], part), 71), part)
    keys = draw_keys(jax.random.fold_in(jax.random.fold_in(splits[13], part), 71), part)
    values = scatter_about(part_splits[2], (TOKENS, KV_HEADS * HEAD), 6.0, 24.0, ((0, 4), (1, 4)))
    teacher_residual = draw_teacher_residual(jax.random.fold_in(jax.random.fold_in(splits[13], part), 71), part)
    teacher_out = scatter_about(splits[4], (HEADS * HEAD, TD), (HEADS * HEAD) ** -0.5, 0.09375, ((0, 4), (1, 4)))
    teacher_gain = jnp.clip(1.0 + 0.18 * jax.random.normal(splits[5], (TD,), jnp.float32), 0.1, 1.9)
    projector = scatter_about(splits[6], (TD, SD), TD ** -0.5, 0.0625, ((0, 4),))
    span_starts = draw_span_starts(jax.random.fold_in(jax.random.fold_in(splits[13], part), 71), part)
    span_ends = draw_span_ends(jax.random.fold_in(jax.random.fold_in(splits[13], part), 71), part)
    aligned_counts = draw_aligned_counts(jax.random.fold_in(jax.random.fold_in(splits[13], part), 71), part)
    student_context = scatter_about(part_splits[10], (TOKENS, SD), 0.125, 0.75, ((0, 4), (1, 4)))
    student_out = scatter_about(splits[11], (SD, SD), SD ** -0.5, 0.109375, ((0, 4),))
    student_residual = scatter_about(part_splits[12], (TOKENS, SD), 0.25, 1.5, ((0, 4), (1, 4)))
    return {"queries": queries, "keys": keys, "values": values, "teacher_residual": teacher_residual, "teacher_out": teacher_out, "teacher_gain": teacher_gain, "projector": projector, "span_starts": span_starts, "span_ends": span_ends, "aligned_counts": aligned_counts, "student_context": student_context, "student_out": student_out, "student_residual": student_residual}


def attend_heads(queries, keys, values):
    per_key = HEADS // KV_HEADS
    positions = jnp.arange(TOKENS, dtype=jnp.int32)
    causal = positions[None, :] <= positions[:, None]
    score_scale = 1.0 / math.sqrt(HEAD)

    def one_head(head_index):
        key_head = head_index // per_key
        query_columns = lax.dynamic_slice_in_dim(queries, (head_index * HEAD).astype(jnp.int32), HEAD, 1)
        key_columns = lax.dynamic_slice_in_dim(keys, (key_head * HEAD).astype(jnp.int32), HEAD, 1)
        value_columns = lax.dynamic_slice_in_dim(values, (key_head * HEAD).astype(jnp.int32), HEAD, 1)
        scores = jnp.dot(query_columns, key_columns.T, preferred_element_type=jnp.float32) * score_scale
        scores = jnp.where(causal, scores, -jnp.inf)
        row_max = lax.optimization_barrier(jnp.max(scores, axis=1, keepdims=True))
        exponent = jnp.exp(scores - row_max)
        row_total = lax.optimization_barrier(jnp.sum(exponent, axis=1, keepdims=True))
        weights = exponent.astype(jnp.bfloat16)
        mixed_values = jnp.dot(weights, value_columns, preferred_element_type=jnp.float32)
        return (mixed_values / row_total).astype(jnp.bfloat16)
    heads_out = lax.map(one_head, jnp.arange(HEADS, dtype=jnp.int32))
    return jnp.transpose(heads_out, (1, 0, 2)).reshape(TOKENS, HEADS * HEAD)

def project_heads(attended, teacher_out):
    group_width = HEADS * HEAD // N_TP
    grouped = attended.reshape(TOKENS, N_TP, group_width).transpose(1, 0, 2)
    weight_groups = teacher_out.reshape(N_TP, group_width, TD)

    def add_group(running, operands):
        partial_sum = jnp.dot(operands[0], operands[1], preferred_element_type=jnp.float32).astype(jnp.bfloat16)
        partial_sum = lax.optimization_barrier(partial_sum)
        return (running + partial_sum.astype(jnp.float32), None)
    mixed_heads, _ = lax.scan(add_group, jnp.zeros((TOKENS, TD), jnp.float32), (grouped, weight_groups))
    return mixed_heads

def pool_spans(normed, span_starts, span_ends):
    positions = jnp.arange(TOKENS, dtype=jnp.int32)
    padded = jnp.pad(normed.astype(jnp.float32), ((HALO, HALO), (0, 0)))
    pooled = jnp.zeros((TOKENS, TD), jnp.float32)
    for offset in range(-HALO, HALO + 1):
        teacher_rows = positions + offset
        inside = (teacher_rows >= span_starts) & (teacher_rows < span_ends)
        shifted = padded[HALO + offset:HALO + offset + TOKENS]
        pooled = pooled + jnp.where(inside[:, None], shifted, 0.0)
    lengths = (span_ends - span_starts).astype(jnp.float32)
    return (pooled / lengths[:, None]).astype(jnp.bfloat16)

def reference(queries, keys, values, teacher_residual, teacher_out, teacher_gain, projector, span_starts, span_ends, aligned_counts, student_context, student_out, student_residual):
    attended = attend_heads(queries, keys, values)
    hidden = teacher_residual.astype(jnp.float32) + project_heads(attended, teacher_out)
    mean_square = lax.optimization_barrier(jnp.mean(hidden * hidden, axis=1, keepdims=True))
    normed = (hidden * lax.rsqrt(mean_square + 1e-06) * teacher_gain.astype(jnp.float32)).astype(jnp.bfloat16)
    pooled = pool_spans(normed, span_starts, span_ends)
    target = jnp.dot(pooled, projector, preferred_element_type=jnp.float32)
    student_hidden = student_residual.astype(jnp.float32) + jnp.dot(student_context, student_out, preferred_element_type=jnp.float32)
    positions = jnp.arange(TOKENS, dtype=jnp.int32)
    shard_counts = jnp.repeat(aligned_counts, TOK_DEV)
    valid_rows = positions % TOK_DEV < shard_counts
    grad_hidden = jnp.where(valid_rows[:, None], student_hidden - target, 0.0).astype(jnp.bfloat16)
    grad_context = jnp.dot(grad_hidden, student_out.T, preferred_element_type=jnp.float32).astype(jnp.bfloat16)
    grad_out = jnp.dot(student_context.T, grad_hidden, preferred_element_type=jnp.float32)
    return (grad_out, grad_context)
```

```python
import math

import jax
import jax.numpy as jnp
from jax import lax
from jax.sharding import PartitionSpec as P

TD = 8192
HEADS = 32
KV_HEADS = 8
HEAD = 128
HALO = 16


def padded(cells, sides, width):
    for axis, dim in sides:
        count = lax.axis_size(axis)
        ends = count - 1
        head = lax.slice_in_dim(cells, 0, width, axis=dim)
        tail = lax.slice_in_dim(cells, cells.shape[dim] - width, cells.shape[dim], axis=dim)
        cells = jnp.concatenate(
            [
                lax.ppermute(tail, axis, [(i, (i + 1) % count) for i in range(ends)]),
                cells,
                lax.ppermute(head, axis, [((i + 1) % count, i) for i in range(ends)]),
            ],
            axis=dim,
        )
    return cells


def attend_local(queries, keys, values):
    row_count = queries.shape[0]
    key_heads = keys.shape[1] // HEAD
    per_key = HEADS // KV_HEADS
    score_scale = 1.0 / math.sqrt(HEAD)
    query_grid = queries.reshape(row_count, key_heads, per_key, HEAD)
    query_position = lax.axis_index("ctx") * row_count + jnp.arange(row_count, dtype=jnp.int32)
    row_max = jnp.full((key_heads, per_key, row_count), -1e30, jnp.float32)
    key_piece = lax.all_gather(keys, "ctx", axis=0, tiled=True)
    value_piece = lax.all_gather(values, "ctx", axis=0, tiled=True)
    piece_rows = key_piece.shape[0]
    key_grid = key_piece.reshape(piece_rows, key_heads, HEAD)
    value_grid = value_piece.reshape(piece_rows, key_heads, HEAD)
    scores = (
        jnp.einsum("qkgd,ckd->kgqc", query_grid, key_grid, preferred_element_type=jnp.float32)
        * score_scale
    )
    key_position = jnp.arange(piece_rows, dtype=jnp.int32)
    allowed = key_position[None, :] <= query_position[:, None]
    scores = jnp.where(allowed, scores, -jnp.inf)
    new_max = jnp.maximum(row_max, jnp.max(scores, axis=3))
    exponent = jnp.exp(scores - new_max[..., None])
    row_total = jnp.sum(exponent, axis=3)
    mixed_values = jnp.einsum(
        "kgqc,ckd->kgqd",
        exponent.astype(jnp.bfloat16),
        value_grid,
        preferred_element_type=jnp.float32,
    )
    weighted = mixed_values
    row_max, row_total, weighted = (new_max, row_total, weighted)
    attended = (weighted / row_total[..., None]).astype(jnp.bfloat16)
    return jnp.transpose(attended, (2, 0, 1, 3)).reshape(row_count, key_heads * per_key * HEAD)


def body(
    queries,
    keys,
    values,
    teacher_residual,
    teacher_out,
    teacher_gain,
    projector,
    span_starts,
    span_ends,
    aligned_counts,
    student_context,
    student_out,
    student_residual,
):
    attended = attend_local(queries, keys, values)
    row_count = attended.shape[0]
    feature_width = teacher_residual.shape[1]
    column_terms = jnp.dot(
        attended,
        lax.all_gather(teacher_out, "ctx", axis=1, tiled=True),
        preferred_element_type=jnp.float32,
    )
    summed = lax.psum_scatter(
        column_terms.astype(jnp.bfloat16), "tp", scatter_dimension=1, tiled=True
    ).astype(jnp.float32)
    hidden = teacher_residual.astype(jnp.float32) + summed
    squares = lax.psum(jnp.sum(hidden * hidden, axis=1), "tp")
    gain_share = lax.dynamic_slice_in_dim(
        teacher_gain, lax.axis_index("tp") * feature_width, feature_width, 0
    )
    normed = (hidden * lax.rsqrt(squares[:, None] / TD + 1e-06) * gain_share).astype(jnp.bfloat16)
    extended = padded(normed, (("ctx", 0),), HALO)
    teacher_position = (
        lax.axis_index("ctx") * row_count - HALO + jnp.arange(row_count + 2 * HALO, dtype=jnp.int32)
    )
    inside = (teacher_position[None, :] >= span_starts[:, None]) & (
        teacher_position[None, :] < span_ends[:, None]
    )
    span_sums = jnp.dot(inside.astype(jnp.bfloat16), extended, preferred_element_type=jnp.float32)
    lengths = (span_ends - span_starts).astype(jnp.float32)
    pooled = (span_sums / lengths[:, None]).astype(jnp.bfloat16)
    student_term = jnp.dot(student_context, student_out, preferred_element_type=jnp.float32)
    target_term = jnp.dot(pooled, projector, preferred_element_type=jnp.float32)
    residual_gap = lax.psum_scatter(
        (student_term - target_term).astype(jnp.bfloat16), "tp", scatter_dimension=1, tiled=True
    ).astype(jnp.float32)
    local_rows = jnp.arange(row_count, dtype=jnp.int32)
    valid_rows = local_rows < aligned_counts[0]
    grad_hidden = jnp.where(
        valid_rows[:, None], student_residual.astype(jnp.float32) + residual_gap, 0.0
    ).astype(jnp.bfloat16)
    grad_full = lax.all_gather(grad_hidden, "tp", axis=1, tiled=True)
    grad_context = lax.dot_general(
        grad_full, student_out, (((1,), (1,)), ((), ())), preferred_element_type=jnp.float32
    ).astype(jnp.bfloat16)
    context_rows = lax.all_gather(student_context, "ctx", axis=0, tiled=True)
    grad_columns = lax.all_to_all(grad_full, "ctx", split_axis=1, concat_axis=0, tiled=True)
    grad_out = lax.dot_general(
        context_rows, grad_columns, (((0,), (0,)), ((), ())), preferred_element_type=jnp.float32
    )
    return (grad_out, grad_context)


def solution(mesh):
    return jax.shard_map(
        body,
        mesh=mesh,
        in_specs=(
            P(("groups", "ctx"), "tp"),
            P(("groups", "ctx"), "tp"),
            P(("groups", "ctx"), "tp"),
            P(("groups", "ctx"), "tp"),
            P("tp", "ctx"),
            P(),
            P("tp", None),
            P(("groups", "ctx")),
            P(("groups", "ctx")),
            P(("groups", "ctx")),
            P(("groups", "ctx"), "tp"),
            P("tp", None),
            P(("groups", "ctx"), "tp"),
        ),
        out_specs=(P(("groups", "tp"), "ctx"), P(("groups", "ctx"), "tp")),
        check_vma=False,
    )
```

```python
import math

import jax
import jax.numpy as jnp
from jax import lax
from jax.experimental import pallas as pl
from jax.experimental.pallas import tpu as pltpu
from jax.sharding import PartitionSpec as P

TD = 8192
HEADS = 32
KV_HEADS = 8
HEAD = 128
HALO = 16


def padded(cells, sides, width):
    for axis, dim in sides:
        count = lax.axis_size(axis)
        ends = count - 1
        head = lax.slice_in_dim(cells, 0, width, axis=dim)
        tail = lax.slice_in_dim(cells, cells.shape[dim] - width, cells.shape[dim], axis=dim)
        cells = jnp.concatenate(
            [
                lax.ppermute(tail, axis, [(i, (i + 1) % count) for i in range(ends)]),
                cells,
                lax.ppermute(head, axis, [((i + 1) % count, i) for i in range(ends)]),
            ],
            axis=dim,
        )
    return cells


def attend_local(queries, keys, values):
    row_count = queries.shape[0]
    key_heads = keys.shape[1] // HEAD
    per_key = HEADS // KV_HEADS
    score_scale = 1.0 / math.sqrt(HEAD)
    query_grid = queries.reshape(row_count, key_heads, per_key, HEAD)
    query_position = lax.axis_index("ctx") * row_count + jnp.arange(row_count, dtype=jnp.int32)
    row_max = jnp.full((key_heads, per_key, row_count), -1e30, jnp.float32)
    key_piece = lax.all_gather(keys, "ctx", axis=0, tiled=True)
    value_piece = lax.all_gather(values, "ctx", axis=0, tiled=True)
    piece_rows = key_piece.shape[0]
    key_grid = key_piece.reshape(piece_rows, key_heads, HEAD)
    value_grid = value_piece.reshape(piece_rows, key_heads, HEAD)
    scores = (
        jnp.einsum("qkgd,ckd->kgqc", query_grid, key_grid, preferred_element_type=jnp.float32)
        * score_scale
    )
    key_position = jnp.arange(piece_rows, dtype=jnp.int32)
    allowed = key_position[None, :] <= query_position[:, None]
    scores = jnp.where(allowed, scores, -jnp.inf)
    new_max = jnp.maximum(row_max, jnp.max(scores, axis=3))
    exponent = jnp.exp(scores - new_max[..., None])
    row_total = jnp.sum(exponent, axis=3)
    mixed_values = jnp.einsum(
        "kgqc,ckd->kgqd",
        exponent.astype(jnp.bfloat16),
        value_grid,
        preferred_element_type=jnp.float32,
    )
    weighted = mixed_values
    row_max, row_total, weighted = (new_max, row_total, weighted)
    attended = (weighted / row_total[..., None]).astype(jnp.bfloat16)
    return jnp.transpose(attended, (2, 0, 1, 3)).reshape(row_count, key_heads * per_key * HEAD)


CHUNKS = 8
MESH = pl.DeviceIdType.MESH


def project_kernel(
    q_ref, k_ref, v_ref, res_ref, own_ref, out_ref,
    kv, weights, attended, peak, total, mixed, sends, lands, far_lands,
    kv_send, kv_recv, x_send, x_recv, s_send, s_recv, y_send, y_recv, f_send, f_recv,
    z_send, z_recv, far_recv,
):
    group = lax.axis_index("groups")
    c = lax.axis_index("ctx")
    t = lax.axis_index("tp")
    last = lax.axis_size("tp") - 1
    x, core = c // 2, c % 2
    sibling = {"ctx": 2 * x + 1 - core}
    across = {"ctx": 2 * (1 - x) + core}
    twin = {"groups": 1 - group}
    dests = (c, 2 * x + 1 - core, 2 * (1 - x) + core, 2 * (1 - x) + 1 - core)
    rows = q_ref.shape[0]
    depth, width = own_ref.shape
    cut = width // CHUNKS
    half = depth // 2
    groups_of = q_ref.shape[1] // k_ref.shape[1]
    key_heads = k_ref.shape[1] // HEAD

    barrier = pltpu.get_barrier_semaphore()
    for peer in (sibling, across, twin):
        pl.semaphore_signal(barrier, inc=1, device_id=peer, device_id_type=MESH)

    @pl.when(t > 0)
    def _():
        pl.semaphore_signal(barrier, inc=1, device_id={"tp": t - 1}, device_id_type=MESH)

    @pl.when(t < last)
    def _():
        pl.semaphore_signal(barrier, inc=1, device_id={"tp": t + 1}, device_id_type=MESH)

    pl.semaphore_wait(barrier, 3 + (t > 0).astype(jnp.int32) + (t < last).astype(jnp.int32))

    def remote(src, dst, send_sem, recv_sem, peer):
        return pltpu.make_async_remote_copy(
            src_ref=src, dst_ref=dst, send_sem=send_sem, recv_sem=recv_sem,
            device_id=peer, device_id_type=MESH,
        )

    def kv_copy(slot, part, src, peer):
        return remote(src, kv.at[slot, part], kv_send.at[slot, part], kv_recv.at[slot, part], peer)

    def columns(j):
        return pl.ds(pl.multiple_of(j * cut, cut), cut)

    def half_rows(which):
        return pl.ds(pl.multiple_of(which * half, half), half)

    def across_copy(j):
        where = (half_rows(group), columns(j))
        return remote(
            own_ref.at[where], weights.at[(1,) + where], x_send.at[j], x_recv.at[j], across
        )

    def sibling_copy(j):
        where = (slice(None), columns(j))
        return remote(
            own_ref.at[where], weights.at[(0,) + where], s_send.at[j], s_recv.at[j], sibling
        )

    def twin_copy(j, which):
        where = (1, half_rows(which), columns(j))
        return remote(weights.at[where], weights.at[where], y_send.at[j], y_recv.at[j], twin)

    def forward_copy(j, order, which):
        where = (half_rows(which), columns(j))
        return remote(
            weights.at[(1,) + where], weights.at[(2,) + where],
            f_send.at[order, j], f_recv.at[order, j], sibling,
        )

    own_kv = (k_ref, v_ref)

    @pl.when(x == 0)
    def _():
        for part in range(2):
            kv_copy(1, part, own_kv[part], across).start()

    @pl.when(core == 0)
    def _():
        for part in range(2):
            kv_copy(0, part, own_kv[part], sibling).start()

    for j in range(2):
        across_copy(j).start()
        sibling_copy(j).start()

    def block_scores(head, keys):
        stacked = jnp.concatenate(
            [
                q_ref[:, (head * groups_of + g) * HEAD:(head * groups_of + g + 1) * HEAD]
                for g in range(groups_of)
            ],
            axis=0,
        )
        return lax.dot_general(
            stacked, keys, (((1,), (1,)), ((), ())), preferred_element_type=jnp.float32
        ) * (1.0 / math.sqrt(HEAD))

    for head in range(key_heads):
        lanes = slice(head * HEAD, (head + 1) * HEAD)
        scores = block_scores(head, k_ref[:, lanes])
        query_row = lax.broadcasted_iota(jnp.int32, scores.shape, 0) % rows
        key_row = lax.broadcasted_iota(jnp.int32, scores.shape, 1)
        scores = jnp.where(key_row <= query_row, scores, -1e30)
        top = jnp.max(scores, axis=1, keepdims=True)
        exponent = jnp.exp(scores - top)
        peak[head] = top
        total[head] = jnp.sum(exponent, axis=1, keepdims=True)
        mixed[head] = jnp.dot(
            exponent.astype(jnp.bfloat16), v_ref[:, lanes], preferred_element_type=jnp.float32
        )

    def add_block(slot):
        for head in range(key_heads):
            lanes = slice(head * HEAD, (head + 1) * HEAD)
            scores = block_scores(head, kv[slot, 0, :, lanes])
            top = jnp.maximum(peak[head], jnp.max(scores, axis=1, keepdims=True))
            shrink = jnp.exp(peak[head] - top)
            exponent = jnp.exp(scores - top)
            peak[head] = top
            total[head] = total[head] * shrink + jnp.sum(exponent, axis=1, keepdims=True)
            mixed[head] = mixed[head] * shrink + jnp.dot(
                exponent.astype(jnp.bfloat16), kv[slot, 1, :, lanes],
                preferred_element_type=jnp.float32,
            )

    @pl.when(core == 1)
    def _():
        for part in range(2):
            kv_copy(0, part, own_kv[part], sibling).wait_recv()
        add_block(0)

    @pl.when(x == 1)
    def _():
        for part in range(2):
            kv_copy(1, part, own_kv[part], across).wait_recv()
        for part in range(2):
            kv_copy(2, part, kv.at[1, part], sibling).start()
        add_block(1)
        for part in range(2):
            kv_copy(2, part, kv.at[1, part], sibling).wait_recv()
        add_block(2)

    for j in range(2, CHUNKS):
        across_copy(j).start()
        sibling_copy(j).start()

    for head in range(key_heads):
        result = (mixed[head] / total[head]).astype(jnp.bfloat16)
        for g in range(groups_of):
            at = (head * groups_of + g) * HEAD
            attended[:, at:at + HEAD] = result[g * rows:(g + 1) * rows]

    def z_copy(i, j, peer):
        return remote(
            sends.at[i, j], lands.at[i, j], z_send.at[i, j], z_recv.at[i, j], {"tp": peer}
        )

    def far_copy(i, j, peer):
        return remote(
            sends.at[i, j], far_lands.at[j], z_send.at[i, j], far_recv.at[j], {"tp": peer}
        )

    def process(i, j, block):
        dest = dests[i]
        product = jnp.dot(attended[...], block, preferred_element_type=jnp.float32)
        towards = jnp.where(dest > t, t + 1, t - 1)
        incoming = ((dest > t) & (t > 0)) | ((dest < t) & (t < last))

        @pl.when(dest == t)
        def _():
            out_ref[:, columns(j)] = product + res_ref[:, columns(j)].astype(jnp.float32)

        @pl.when((dest != t) & incoming)
        def _():
            z_copy(i, j, towards).wait_recv()
            sends[i, j] = (product + lands[i, j].astype(jnp.float32)).astype(jnp.bfloat16)

        @pl.when((dest != t) & jnp.logical_not(incoming))
        def _():
            sends[i, j] = product.astype(jnp.bfloat16)

        @pl.when((dest != t) & (dest != t - 1))
        def _():
            z_copy(i, j, towards).start()

        @pl.when(dest == t - 1)
        def _():
            far_copy(i, j, towards).start()

    def step(j, carry):
        @pl.when(j < CHUNKS)
        def _():
            process(0, j, own_ref[:, columns(j)])
            sibling_copy(j).wait_recv()
            process(1, j, weights[0, :, columns(j)])
            across_copy(j).wait_recv()
            twin_copy(j, group).start()
            forward_copy(j, 0, group).start()

        @pl.when(j > 0)
        def _():
            p = j - 1
            twin_copy(p, 1 - group).wait_recv()
            forward_copy(p, 1, 1 - group).start()
            process(2, p, weights[1, :, columns(p)])
            forward_copy(p, 0, group).wait_recv()
            forward_copy(p, 1, 1 - group).wait_recv()
            process(3, p, weights[2, :, columns(p)])

        return carry

    lax.fori_loop(0, CHUNKS + 1, step, 0)

    def finish(j, carry):
        for i in range(4):
            @pl.when((dests[i] == t) & (t > 0))
            def _():
                z_copy(i, j, t).wait_recv()
                out_ref[:, columns(j)] += lands[i, j].astype(jnp.float32)

        @pl.when(t < last)
        def _():
            far_copy(0, j, t).wait_recv()
            out_ref[:, columns(j)] += far_lands[j].astype(jnp.float32)

        return carry

    lax.fori_loop(0, CHUNKS, finish, 0)

    def drain(j, carry):
        across_copy(j).wait_send()
        sibling_copy(j).wait_send()
        twin_copy(j, group).wait_send()
        forward_copy(j, 0, group).wait_send()
        forward_copy(j, 1, 1 - group).wait_send()
        for i in range(4):
            @pl.when(dests[i] != t)
            def _():
                z_copy(i, j, t).wait_send()
        return carry

    lax.fori_loop(0, CHUNKS, drain, 0)

    @pl.when(x == 0)
    def _():
        for part in range(2):
            kv_copy(1, part, own_kv[part], across).wait_send()

    @pl.when(core == 0)
    def _():
        for part in range(2):
            kv_copy(0, part, own_kv[part], sibling).wait_send()

    @pl.when(x == 1)
    def _():
        for part in range(2):
            kv_copy(2, part, kv.at[1, part], sibling).wait_send()


def hidden_fused(queries, keys, values, teacher_residual, teacher_out):
    rows, key_width = keys.shape
    depth, width = teacher_out.shape
    cut = width // CHUNKS
    key_heads = key_width // HEAD
    stacked = rows * queries.shape[1] // key_width
    dma = pltpu.SemaphoreType.DMA
    vmem = pl.BlockSpec(memory_space=pltpu.VMEM)
    return pl.pallas_call(
        project_kernel,
        out_shape=jax.ShapeDtypeStruct((rows, width), jnp.float32),
        in_specs=[vmem] * 5,
        out_specs=vmem,
        scratch_shapes=[
            pltpu.VMEM((3, 2, rows, key_width), jnp.bfloat16),
            pltpu.VMEM((3, depth, width), jnp.bfloat16),
            pltpu.VMEM((rows, depth), jnp.bfloat16),
            pltpu.VMEM((key_heads, stacked, 1), jnp.float32),
            pltpu.VMEM((key_heads, stacked, 1), jnp.float32),
            pltpu.VMEM((key_heads, stacked, HEAD), jnp.float32),
            pltpu.VMEM((4, CHUNKS, rows, cut), jnp.bfloat16),
            pltpu.VMEM((4, CHUNKS, rows, cut), jnp.bfloat16),
            pltpu.VMEM((CHUNKS, rows, cut), jnp.bfloat16),
            dma((3, 2)), dma((3, 2)),
            dma((CHUNKS,)), dma((CHUNKS,)),
            dma((CHUNKS,)), dma((CHUNKS,)),
            dma((CHUNKS,)), dma((CHUNKS,)),
            dma((2, CHUNKS)), dma((2, CHUNKS)),
            dma((4, CHUNKS)), dma((4, CHUNKS)),
            dma((CHUNKS,)),
        ],
        compiler_params=pltpu.CompilerParams(
            collective_id=0, has_side_effects=True, vmem_limit_bytes=48 * 1024 * 1024
        ),
    )(queries, keys, values, teacher_residual, teacher_out)


def hidden_plain(queries, keys, values, teacher_residual, teacher_out):
    attended = attend_local(queries, keys, values)
    column_terms = jnp.dot(
        attended,
        lax.all_gather(teacher_out, "ctx", axis=1, tiled=True),
        preferred_element_type=jnp.float32,
    )
    summed = lax.psum_scatter(
        column_terms.astype(jnp.bfloat16), "tp", scatter_dimension=1, tiled=True
    ).astype(jnp.float32)
    return teacher_residual.astype(jnp.float32) + summed


def body(
    queries,
    keys,
    values,
    teacher_residual,
    teacher_out,
    teacher_gain,
    projector,
    span_starts,
    span_ends,
    aligned_counts,
    student_context,
    student_out,
    student_residual,
):
    sizes = (lax.axis_size("groups"), lax.axis_size("ctx"), lax.axis_size("tp"))
    hidden_of = hidden_fused if sizes == (2, 4, 4) else hidden_plain
    hidden = hidden_of(queries, keys, values, teacher_residual, teacher_out)
    row_count, feature_width = teacher_residual.shape
    squares = lax.psum(jnp.sum(hidden * hidden, axis=1), "tp")
    gain_share = lax.dynamic_slice_in_dim(
        teacher_gain, lax.axis_index("tp") * feature_width, feature_width, 0
    )
    normed = (hidden * lax.rsqrt(squares[:, None] / TD + 1e-06) * gain_share).astype(jnp.bfloat16)
    extended = padded(normed, (("ctx", 0),), HALO)
    teacher_position = (
        lax.axis_index("ctx") * row_count - HALO + jnp.arange(row_count + 2 * HALO, dtype=jnp.int32)
    )
    inside = (teacher_position[None, :] >= span_starts[:, None]) & (
        teacher_position[None, :] < span_ends[:, None]
    )
    span_sums = jnp.dot(inside.astype(jnp.bfloat16), extended, preferred_element_type=jnp.float32)
    lengths = (span_ends - span_starts).astype(jnp.float32)
    pooled = (span_sums / lengths[:, None]).astype(jnp.bfloat16)
    student_term = jnp.dot(student_context, student_out, preferred_element_type=jnp.float32)
    target_term = jnp.dot(pooled, projector, preferred_element_type=jnp.float32)
    residual_gap = lax.psum_scatter(
        (student_term - target_term).astype(jnp.bfloat16), "tp", scatter_dimension=1, tiled=True
    ).astype(jnp.float32)
    local_rows = jnp.arange(row_count, dtype=jnp.int32)
    valid_rows = local_rows < aligned_counts[0]
    grad_hidden = jnp.where(
        valid_rows[:, None], student_residual.astype(jnp.float32) + residual_gap, 0.0
    ).astype(jnp.bfloat16)
    grad_full = lax.all_gather(grad_hidden, "tp", axis=1, tiled=True)
    grad_context = lax.dot_general(
        grad_full, student_out, (((1,), (1,)), ((), ())), preferred_element_type=jnp.float32
    ).astype(jnp.bfloat16)
    context_rows = lax.all_gather(student_context, "ctx", axis=0, tiled=True)
    grad_columns = lax.all_to_all(grad_full, "ctx", split_axis=1, concat_axis=0, tiled=True)
    grad_out = lax.dot_general(
        context_rows, grad_columns, (((0,), (0,)), ((), ())), preferred_element_type=jnp.float32
    )
    return (grad_out, grad_context)


def solution(mesh):
    return jax.shard_map(
        body,
        mesh=mesh,
        in_specs=(
            P(("groups", "ctx"), "tp"),
            P(("groups", "ctx"), "tp"),
            P(("groups", "ctx"), "tp"),
            P(("groups", "ctx"), "tp"),
            P("tp", "ctx"),
            P(),
            P("tp", None),
            P(("groups", "ctx")),
            P(("groups", "ctx")),
            P(("groups", "ctx")),
            P(("groups", "ctx"), "tp"),
            P("tp", None),
            P(("groups", "ctx"), "tp"),
        ),
        out_specs=(P(("groups", "tp"), "ctx"), P(("groups", "ctx"), "tp")),
        check_vma=False,
    )
```

```python
import math

import jax
import jax.numpy as jnp
from jax import lax
from jax.experimental import pallas as pl
from jax.experimental.pallas import tpu as pltpu
from jax.sharding import PartitionSpec as P

TD = 8192
HEADS = 32
KV_HEADS = 8
HEAD = 128
HALO = 16


def padded(cells, sides, width):
    for axis, dim in sides:
        count = lax.axis_size(axis)
        ends = count - 1
        head = lax.slice_in_dim(cells, 0, width, axis=dim)
        tail = lax.slice_in_dim(cells, cells.shape[dim] - width, cells.shape[dim], axis=dim)
        cells = jnp.concatenate(
            [
                lax.ppermute(tail, axis, [(i, (i + 1) % count) for i in range(ends)]),
                cells,
                lax.ppermute(head, axis, [((i + 1) % count, i) for i in range(ends)]),
            ],
            axis=dim,
        )
    return cells


def attend_local(queries, keys, values):
    row_count = queries.shape[0]
    key_heads = keys.shape[1] // HEAD
    per_key = HEADS // KV_HEADS
    score_scale = 1.0 / math.sqrt(HEAD)
    query_grid = queries.reshape(row_count, key_heads, per_key, HEAD)
    query_position = lax.axis_index("ctx") * row_count + jnp.arange(row_count, dtype=jnp.int32)
    row_max = jnp.full((key_heads, per_key, row_count), -1e30, jnp.float32)
    key_piece = lax.all_gather(keys, "ctx", axis=0, tiled=True)
    value_piece = lax.all_gather(values, "ctx", axis=0, tiled=True)
    piece_rows = key_piece.shape[0]
    key_grid = key_piece.reshape(piece_rows, key_heads, HEAD)
    value_grid = value_piece.reshape(piece_rows, key_heads, HEAD)
    scores = (
        jnp.einsum("qkgd,ckd->kgqc", query_grid, key_grid, preferred_element_type=jnp.float32)
        * score_scale
    )
    key_position = jnp.arange(piece_rows, dtype=jnp.int32)
    allowed = key_position[None, :] <= query_position[:, None]
    scores = jnp.where(allowed, scores, -jnp.inf)
    new_max = jnp.maximum(row_max, jnp.max(scores, axis=3))
    exponent = jnp.exp(scores - new_max[..., None])
    row_total = jnp.sum(exponent, axis=3)
    mixed_values = jnp.einsum(
        "kgqc,ckd->kgqd",
        exponent.astype(jnp.bfloat16),
        value_grid,
        preferred_element_type=jnp.float32,
    )
    weighted = mixed_values
    row_max, row_total, weighted = (new_max, row_total, weighted)
    attended = (weighted / row_total[..., None]).astype(jnp.bfloat16)
    return jnp.transpose(attended, (2, 0, 1, 3)).reshape(row_count, key_heads * per_key * HEAD)


CHUNKS = 8
MESH = pl.DeviceIdType.MESH


def project_kernel(
    q_ref, k_ref, v_ref, res_ref, own_ref, out_ref,
    kv, weights, attended, peak, total, mixed, sends, lands, far_lands,
    kv_send, kv_recv, x_send, x_recv, s_send, s_recv, y_send, y_recv, f_send, f_recv,
    z_send, z_recv, far_recv,
):
    group = lax.axis_index("groups")
    c = lax.axis_index("ctx")
    t = lax.axis_index("tp")
    last = lax.axis_size("tp") - 1
    x, core = c // 2, c % 2
    sibling = {"ctx": 2 * x + 1 - core}
    across = {"ctx": 2 * (1 - x) + core}
    twin = {"groups": 1 - group}
    dests = (c, 2 * x + 1 - core, 2 * (1 - x) + core, 2 * (1 - x) + 1 - core)
    rows = q_ref.shape[0]
    depth, width = own_ref.shape
    cut = width // CHUNKS
    half = depth // 2
    groups_of = q_ref.shape[1] // k_ref.shape[1]
    key_heads = k_ref.shape[1] // HEAD

    barrier = pltpu.get_barrier_semaphore()
    for peer in (sibling, across, twin):
        pl.semaphore_signal(barrier, inc=1, device_id=peer, device_id_type=MESH)

    @pl.when(t > 0)
    def _():
        pl.semaphore_signal(barrier, inc=1, device_id={"tp": t - 1}, device_id_type=MESH)

    @pl.when(t < last)
    def _():
        pl.semaphore_signal(barrier, inc=1, device_id={"tp": t + 1}, device_id_type=MESH)

    pl.semaphore_wait(barrier, 3 + (t > 0).astype(jnp.int32) + (t < last).astype(jnp.int32))

    def remote(src, dst, send_sem, recv_sem, peer):
        return pltpu.make_async_remote_copy(
            src_ref=src, dst_ref=dst, send_sem=send_sem, recv_sem=recv_sem,
            device_id=peer, device_id_type=MESH,
        )

    def kv_copy(slot, part, src, peer):
        return remote(src, kv.at[slot, part], kv_send.at[slot, part], kv_recv.at[slot, part], peer)

    def columns(j):
        return pl.ds(pl.multiple_of(j * cut, cut), cut)

    def half_rows(which):
        return pl.ds(pl.multiple_of(which * half, half), half)

    def across_copy(j):
        where = (half_rows(group), columns(j))
        return remote(
            own_ref.at[where], weights.at[(1,) + where], x_send.at[j], x_recv.at[j], across
        )

    def sibling_copy(j):
        where = (slice(None), columns(j))
        return remote(
            own_ref.at[where], weights.at[(0,) + where], s_send.at[j], s_recv.at[j], sibling
        )

    def twin_copy(j, which):
        where = (1, half_rows(which), columns(j))
        return remote(weights.at[where], weights.at[where], y_send.at[j], y_recv.at[j], twin)

    def forward_copy(j, order, which):
        where = (half_rows(which), columns(j))
        return remote(
            weights.at[(1,) + where], weights.at[(2,) + where],
            f_send.at[order, j], f_recv.at[order, j], sibling,
        )

    own_kv = (k_ref, v_ref)

    @pl.when(x == 0)
    def _():
        for part in range(2):
            kv_copy(1, part, own_kv[part], across).start()

    @pl.when(core == 0)
    def _():
        for part in range(2):
            kv_copy(0, part, own_kv[part], sibling).start()

    for j in range(2):
        across_copy(j).start()
        sibling_copy(j).start()

    def block_scores(head, keys):
        stacked = jnp.concatenate(
            [
                q_ref[:, (head * groups_of + g) * HEAD:(head * groups_of + g + 1) * HEAD]
                for g in range(groups_of)
            ],
            axis=0,
        )
        return lax.dot_general(
            stacked, keys, (((1,), (1,)), ((), ())), preferred_element_type=jnp.float32
        ) * (1.0 / math.sqrt(HEAD))

    for head in range(key_heads):
        lanes = slice(head * HEAD, (head + 1) * HEAD)
        scores = block_scores(head, k_ref[:, lanes])
        query_row = lax.broadcasted_iota(jnp.int32, scores.shape, 0) % rows
        key_row = lax.broadcasted_iota(jnp.int32, scores.shape, 1)
        scores = jnp.where(key_row <= query_row, scores, -1e30)
        top = jnp.max(scores, axis=1, keepdims=True)
        exponent = jnp.exp(scores - top)
        peak[head] = top
        total[head] = jnp.sum(exponent, axis=1, keepdims=True)
        mixed[head] = jnp.dot(
            exponent.astype(jnp.bfloat16), v_ref[:, lanes], preferred_element_type=jnp.float32
        )

    def add_block(slot):
        for head in range(key_heads):
            lanes = slice(head * HEAD, (head + 1) * HEAD)
            scores = block_scores(head, kv[slot, 0, :, lanes])
            top = jnp.maximum(peak[head], jnp.max(scores, axis=1, keepdims=True))
            shrink = jnp.exp(peak[head] - top)
            exponent = jnp.exp(scores - top)
            peak[head] = top
            total[head] = total[head] * shrink + jnp.sum(exponent, axis=1, keepdims=True)
            mixed[head] = mixed[head] * shrink + jnp.dot(
                exponent.astype(jnp.bfloat16), kv[slot, 1, :, lanes],
                preferred_element_type=jnp.float32,
            )

    @pl.when(core == 1)
    def _():
        for part in range(2):
            kv_copy(0, part, own_kv[part], sibling).wait_recv()
        add_block(0)

    @pl.when(x == 1)
    def _():
        for part in range(2):
            kv_copy(1, part, own_kv[part], across).wait_recv()
        for part in range(2):
            kv_copy(2, part, kv.at[1, part], sibling).start()
        add_block(1)
        for part in range(2):
            kv_copy(2, part, kv.at[1, part], sibling).wait_recv()
        add_block(2)

    for j in range(2, CHUNKS):
        across_copy(j).start()
        sibling_copy(j).start()

    for head in range(key_heads):
        result = (mixed[head] / total[head]).astype(jnp.bfloat16)
        for g in range(groups_of):
            at = (head * groups_of + g) * HEAD
            attended[:, at:at + HEAD] = result[g * rows:(g + 1) * rows]

    def z_copy(i, j, peer):
        return remote(
            sends.at[i, j], lands.at[i, j], z_send.at[i, j], z_recv.at[i, j], {"tp": peer}
        )

    def far_copy(i, j, peer):
        return remote(
            sends.at[i, j], far_lands.at[j], z_send.at[i, j], far_recv.at[j], {"tp": peer}
        )

    def process(i, j, block):
        dest = dests[i]
        product = jnp.dot(attended[...], block, preferred_element_type=jnp.float32)
        towards = jnp.where(dest > t, t + 1, t - 1)
        incoming = ((dest > t) & (t > 0)) | ((dest < t) & (t < last))

        @pl.when(dest == t)
        def _():
            out_ref[:, columns(j)] = product + res_ref[:, columns(j)].astype(jnp.float32)

        @pl.when((dest != t) & incoming)
        def _():
            z_copy(i, j, towards).wait_recv()
            sends[i, j] = (product + lands[i, j].astype(jnp.float32)).astype(jnp.bfloat16)

        @pl.when((dest != t) & jnp.logical_not(incoming))
        def _():
            sends[i, j] = product.astype(jnp.bfloat16)

        @pl.when((dest != t) & (dest != t - 1))
        def _():
            z_copy(i, j, towards).start()

        @pl.when(dest == t - 1)
        def _():
            far_copy(i, j, towards).start()

    def step(j, carry):
        @pl.when(j < CHUNKS)
        def _():
            process(0, j, own_ref[:, columns(j)])
            sibling_copy(j).wait_recv()
            process(1, j, weights[0, :, columns(j)])
            across_copy(j).wait_recv()
            twin_copy(j, group).start()
            forward_copy(j, 0, group).start()

        @pl.when(j > 0)
        def _():
            p = j - 1
            twin_copy(p, 1 - group).wait_recv()
            forward_copy(p, 1, 1 - group).start()
            process(2, p, weights[1, :, columns(p)])
            forward_copy(p, 0, group).wait_recv()
            forward_copy(p, 1, 1 - group).wait_recv()
            process(3, p, weights[2, :, columns(p)])

        return carry

    lax.fori_loop(0, CHUNKS + 1, step, 0)

    def finish(j, carry):
        for i in range(4):
            @pl.when((dests[i] == t) & (t > 0))
            def _():
                z_copy(i, j, t).wait_recv()
                out_ref[:, columns(j)] += lands[i, j].astype(jnp.float32)

        @pl.when(t < last)
        def _():
            far_copy(0, j, t).wait_recv()
            out_ref[:, columns(j)] += far_lands[j].astype(jnp.float32)

        return carry

    lax.fori_loop(0, CHUNKS, finish, 0)

    def drain(j, carry):
        across_copy(j).wait_send()
        sibling_copy(j).wait_send()
        twin_copy(j, group).wait_send()
        forward_copy(j, 0, group).wait_send()
        forward_copy(j, 1, 1 - group).wait_send()
        for i in range(4):
            @pl.when(dests[i] != t)
            def _():
                z_copy(i, j, t).wait_send()
        return carry

    lax.fori_loop(0, CHUNKS, drain, 0)

    @pl.when(x == 0)
    def _():
        for part in range(2):
            kv_copy(1, part, own_kv[part], across).wait_send()

    @pl.when(core == 0)
    def _():
        for part in range(2):
            kv_copy(0, part, own_kv[part], sibling).wait_send()

    @pl.when(x == 1)
    def _():
        for part in range(2):
            kv_copy(2, part, kv.at[1, part], sibling).wait_send()


def hidden_fused(queries, keys, values, teacher_residual, teacher_out):
    rows, key_width = keys.shape
    depth, width = teacher_out.shape
    cut = width // CHUNKS
    key_heads = key_width // HEAD
    stacked = rows * queries.shape[1] // key_width
    dma = pltpu.SemaphoreType.DMA
    vmem = pl.BlockSpec(memory_space=pltpu.VMEM)
    return pl.pallas_call(
        project_kernel,
        out_shape=jax.ShapeDtypeStruct((rows, width), jnp.float32),
        in_specs=[vmem] * 5,
        out_specs=vmem,
        scratch_shapes=[
            pltpu.VMEM((3, 2, rows, key_width), jnp.bfloat16),
            pltpu.VMEM((3, depth, width), jnp.bfloat16),
            pltpu.VMEM((rows, depth), jnp.bfloat16),
            pltpu.VMEM((key_heads, stacked, 1), jnp.float32),
            pltpu.VMEM((key_heads, stacked, 1), jnp.float32),
            pltpu.VMEM((key_heads, stacked, HEAD), jnp.float32),
            pltpu.VMEM((4, CHUNKS, rows, cut), jnp.bfloat16),
            pltpu.VMEM((4, CHUNKS, rows, cut), jnp.bfloat16),
            pltpu.VMEM((CHUNKS, rows, cut), jnp.bfloat16),
            dma((3, 2)), dma((3, 2)),
            dma((CHUNKS,)), dma((CHUNKS,)),
            dma((CHUNKS,)), dma((CHUNKS,)),
            dma((CHUNKS,)), dma((CHUNKS,)),
            dma((2, CHUNKS)), dma((2, CHUNKS)),
            dma((4, CHUNKS)), dma((4, CHUNKS)),
            dma((CHUNKS,)),
        ],
        compiler_params=pltpu.CompilerParams(
            collective_id=0, has_side_effects=True, vmem_limit_bytes=48 * 1024 * 1024
        ),
    )(queries, keys, values, teacher_residual, teacher_out)


def hidden_plain(queries, keys, values, teacher_residual, teacher_out):
    attended = attend_local(queries, keys, values)
    column_terms = jnp.dot(
        attended,
        lax.all_gather(teacher_out, "ctx", axis=1, tiled=True),
        preferred_element_type=jnp.float32,
    )
    summed = lax.psum_scatter(
        column_terms.astype(jnp.bfloat16), "tp", scatter_dimension=1, tiled=True
    ).astype(jnp.float32)
    return teacher_residual.astype(jnp.float32) + summed


HALVES = 2


def gradient_kernel(
    pooled_ref, proj_ref, sc_ref, so_ref, res_ref, valid_ref, gout_ref, gctx_ref,
    sends, lands, far_lands, gap, grads, crossed, contexts, context_sum,
    z_send, z_recv, far_recv, r_send, r_recv, l_send, l_recv, e_send, e_recv, c_send, c_recv,
):
    c = lax.axis_index("ctx")
    t = lax.axis_index("tp")
    ranks = lax.axis_size("tp")
    last = ranks - 1
    shards = lax.axis_size("ctx")
    block = res_ref.shape[1]
    cut = block // HALVES

    barrier = pltpu.get_barrier_semaphore()
    for peer in range(shards):
        @pl.when(c != peer)
        def _():
            pl.semaphore_signal(barrier, inc=1, device_id={"ctx": peer}, device_id_type=MESH)

    @pl.when(t > 0)
    def _():
        pl.semaphore_signal(barrier, inc=1, device_id={"tp": t - 1}, device_id_type=MESH)

    @pl.when(t < last)
    def _():
        pl.semaphore_signal(barrier, inc=1, device_id={"tp": t + 1}, device_id_type=MESH)

    pl.semaphore_wait(
        barrier, shards - 1 + (t > 0).astype(jnp.int32) + (t < last).astype(jnp.int32)
    )

    def remote(src, dst, send_sem, recv_sem, peer):
        return pltpu.make_async_remote_copy(
            src_ref=src, dst_ref=dst, send_sem=send_sem, recv_sem=recv_sem,
            device_id=peer, device_id_type=MESH,
        )

    def context_copy(sender, peer):
        return remote(
            sc_ref, contexts.at[sender], c_send.at[peer], c_recv.at[sender], {"ctx": peer}
        )

    def z_copy(d, h, peer):
        return remote(
            sends.at[d, h], lands.at[d, h], z_send.at[d, h], z_recv.at[d, h], {"tp": peer}
        )

    def far_copy(d, h, peer):
        return remote(
            sends.at[d, h], far_lands.at[h], z_send.at[d, h], far_recv.at[h], {"tp": peer}
        )

    def right_copy(s, h):
        return remote(
            grads.at[s, h], grads.at[s, h], r_send.at[s, h], r_recv.at[s, h],
            {"tp": jnp.minimum(t + 1, last)},
        )

    def left_copy(s, h):
        return remote(
            grads.at[s, h], grads.at[s, h], l_send.at[s, h], l_recv.at[s, h],
            {"tp": jnp.maximum(t - 1, 0)},
        )

    def cross_copy(s, h, sender):
        return remote(
            grads.at[s, h], crossed.at[sender, h], e_send.at[s, h], e_recv.at[sender, h],
            {"ctx": s},
        )

    for h in range(HALVES):
        for d in (3, 0, 2, 1):
            lanes = slice(d * block + h * cut, d * block + (h + 1) * cut)
            product = jnp.dot(
                sc_ref[...], so_ref[:, lanes], preferred_element_type=jnp.float32
            ) - jnp.dot(pooled_ref[...], proj_ref[:, lanes], preferred_element_type=jnp.float32)
            towards = jnp.where(t < d, t + 1, t - 1)
            incoming = ((t < d) & (t > 0)) | ((t > d) & (t < last))

            @pl.when(t == d)
            def _():
                gap[h] = product

            @pl.when((t != d) & incoming)
            def _():
                z_copy(d, h, towards).wait_recv()
                sends[d, h] = (product + lands[d, h].astype(jnp.float32)).astype(jnp.bfloat16)

            @pl.when((t != d) & jnp.logical_not(incoming))
            def _():
                sends[d, h] = product.astype(jnp.bfloat16)

            @pl.when((t != d) & (t != d + 1))
            def _():
                z_copy(d, h, towards).start()

            @pl.when(t == d + 1)
            def _():
                far_copy(d, h, towards).start()

    for peer in range(shards):
        @pl.when(c != peer)
        def _():
            context_copy(c, peer).start()

    for h in range(HALVES):
        @pl.when(t > 0)
        def _():
            z_copy(t, h, t).wait_recv()
            gap[h] += lands[t, h].astype(jnp.float32)

        @pl.when(t < last)
        def _():
            far_copy(t, h, t).wait_recv()
            gap[h] += far_lands[h].astype(jnp.float32)

        student = res_ref[:, h * cut:(h + 1) * cut].astype(jnp.float32) + gap[h]
        grads[t, h] = jnp.where(valid_ref[...] > 0, student, 0.0).astype(jnp.bfloat16)

        @pl.when(t < last)
        def _():
            right_copy(t, h).start()

        @pl.when(t > 0)
        def _():
            left_copy(t, h).start()

    def cross(s, h):
        @pl.when(s != c)
        def _():
            cross_copy(s, h, c).start()

    def accumulate(s, h):
        lanes = pl.ds(pl.multiple_of(s * block + h * cut, cut), cut)
        context_sum[...] += lax.dot_general(
            grads[s, h], so_ref[:, lanes], (((1,), (1,)), ((), ())),
            preferred_element_type=jnp.float32,
        )

    context_sum[...] = jnp.zeros_like(context_sum)
    for h in range(HALVES):
        cross(t, h)
    for h in range(HALVES):
        accumulate(t, h)
    for hop in range(1, 4):
        for h in range(HALVES):
            @pl.when(t >= hop)
            def _():
                right_copy(t - hop, h).wait_recv()

                @pl.when(t < last)
                def _():
                    right_copy(t - hop, h).start()

                cross(t - hop, h)

            @pl.when(t + hop <= last)
            def _():
                left_copy(t + hop, h).wait_recv()

                @pl.when(t > 0)
                def _():
                    left_copy(t + hop, h).start()

                cross(t + hop, h)

            @pl.when(t >= hop)
            def _():
                accumulate(t - hop, h)

            @pl.when(t + hop <= last)
            def _():
                accumulate(t + hop, h)

    gctx_ref[...] = context_sum[...].astype(jnp.bfloat16)

    def outer(context, grad):
        return lax.dot_general(
            context, grad, (((0,), (0,)), ((), ())), preferred_element_type=jnp.float32
        )

    for h in range(HALVES):
        gout_ref[:, h * cut:(h + 1) * cut] = outer(sc_ref[...], grads[c, h])
    for sender in range(shards):
        @pl.when(c != sender)
        def _():
            context_copy(sender, c).wait_recv()
            for h in range(HALVES):
                cross_copy(c, h, sender).wait_recv()
                gout_ref[:, h * cut:(h + 1) * cut] += outer(contexts[sender], crossed[sender, h])

    for s in range(ranks):
        @pl.when(c != s)
        def _():
            context_copy(c, s).wait_send()

        for h in range(HALVES):
            @pl.when(t != s)
            def _():
                z_copy(s, h, t).wait_send()

            @pl.when(c != s)
            def _():
                cross_copy(s, h, c).wait_send()

            @pl.when((t >= s) & (t < last))
            def _():
                right_copy(s, h).wait_send()

            @pl.when((t <= s) & (t > 0))
            def _():
                left_copy(s, h).wait_send()


def gradients_fused(pooled, projector, student_context, student_out, student_residual, valid_rows):
    rows, block = student_residual.shape
    cut = block // HALVES
    dma = pltpu.SemaphoreType.DMA
    vmem = pl.BlockSpec(memory_space=pltpu.VMEM)
    pieces = pltpu.VMEM((4, HALVES, rows, cut), jnp.bfloat16)
    pair = dma((4, HALVES))
    return pl.pallas_call(
        gradient_kernel,
        out_shape=(
            jax.ShapeDtypeStruct((block, block), jnp.float32),
            jax.ShapeDtypeStruct((rows, block), jnp.bfloat16),
        ),
        in_specs=[vmem] * 6,
        out_specs=(vmem, vmem),
        scratch_shapes=[
            pieces,
            pieces,
            pltpu.VMEM((HALVES, rows, cut), jnp.bfloat16),
            pltpu.VMEM((HALVES, rows, cut), jnp.float32),
            pieces,
            pieces,
            pltpu.VMEM((4, rows, block), jnp.bfloat16),
            pltpu.VMEM((rows, block), jnp.float32),
            pair, pair, dma((HALVES,)), pair, pair, pair, pair, pair, pair, dma((4,)), dma((4,)),
        ],
        compiler_params=pltpu.CompilerParams(
            collective_id=1, has_side_effects=True, vmem_limit_bytes=48 * 1024 * 1024
        ),
    )(
        pooled, projector, student_context, student_out, student_residual,
        valid_rows.astype(jnp.float32)[:, None],
    )


def body(
    queries,
    keys,
    values,
    teacher_residual,
    teacher_out,
    teacher_gain,
    projector,
    span_starts,
    span_ends,
    aligned_counts,
    student_context,
    student_out,
    student_residual,
):
    sizes = (lax.axis_size("groups"), lax.axis_size("ctx"), lax.axis_size("tp"))
    hidden_of = hidden_fused if sizes == (2, 4, 4) else hidden_plain
    hidden = hidden_of(queries, keys, values, teacher_residual, teacher_out)
    row_count, feature_width = teacher_residual.shape
    squares = lax.psum(jnp.sum(hidden * hidden, axis=1), "tp")
    gain_share = lax.dynamic_slice_in_dim(
        teacher_gain, lax.axis_index("tp") * feature_width, feature_width, 0
    )
    normed = (hidden * lax.rsqrt(squares[:, None] / TD + 1e-06) * gain_share).astype(jnp.bfloat16)
    extended = padded(normed, (("ctx", 0),), HALO)
    teacher_position = (
        lax.axis_index("ctx") * row_count - HALO + jnp.arange(row_count + 2 * HALO, dtype=jnp.int32)
    )
    inside = (teacher_position[None, :] >= span_starts[:, None]) & (
        teacher_position[None, :] < span_ends[:, None]
    )
    span_sums = jnp.dot(inside.astype(jnp.bfloat16), extended, preferred_element_type=jnp.float32)
    lengths = (span_ends - span_starts).astype(jnp.float32)
    pooled = (span_sums / lengths[:, None]).astype(jnp.bfloat16)
    valid_rows = jnp.arange(row_count, dtype=jnp.int32) < aligned_counts[0]
    if sizes == (2, 4, 4):
        return gradients_fused(
            pooled, projector, student_context, student_out, student_residual, valid_rows
        )
    student_term = jnp.dot(student_context, student_out, preferred_element_type=jnp.float32)
    target_term = jnp.dot(pooled, projector, preferred_element_type=jnp.float32)
    residual_gap = lax.psum_scatter(
        (student_term - target_term).astype(jnp.bfloat16), "tp", scatter_dimension=1, tiled=True
    ).astype(jnp.float32)
    grad_hidden = jnp.where(
        valid_rows[:, None], student_residual.astype(jnp.float32) + residual_gap, 0.0
    ).astype(jnp.bfloat16)
    grad_full = lax.all_gather(grad_hidden, "tp", axis=1, tiled=True)
    grad_context = lax.dot_general(
        grad_full, student_out, (((1,), (1,)), ((), ())), preferred_element_type=jnp.float32
    ).astype(jnp.bfloat16)
    context_rows = lax.all_gather(student_context, "ctx", axis=0, tiled=True)
    grad_columns = lax.all_to_all(grad_full, "ctx", split_axis=1, concat_axis=0, tiled=True)
    grad_out = lax.dot_general(
        context_rows, grad_columns, (((0,), (0,)), ((), ())), preferred_element_type=jnp.float32
    )
    return (grad_out, grad_context)


def solution(mesh):
    return jax.shard_map(
        body,
        mesh=mesh,
        in_specs=(
            P(("groups", "ctx"), "tp"),
            P(("groups", "ctx"), "tp"),
            P(("groups", "ctx"), "tp"),
            P(("groups", "ctx"), "tp"),
            P("tp", "ctx"),
            P(),
            P("tp", None),
            P(("groups", "ctx")),
            P(("groups", "ctx")),
            P(("groups", "ctx")),
            P(("groups", "ctx"), "tp"),
            P("tp", None),
            P(("groups", "ctx"), "tp"),
        ),
        out_specs=(P(("groups", "tp"), "ctx"), P(("groups", "ctx"), "tp")),
        check_vma=False,
    )
```
